32 devices in a mesh: ctx: 4 (over y, x), head: 8 (over z, core).
Axes of the slice: x: 2, y: 2, z: 4, core: 2. Of those that a mesh axis runs over, the one named last changes fastest.
Arguments:
- passage_q: bfloat16 [4096, 16384], P(('ctx', 'head')), may hold values from -12 to 12
- passage_k: bfloat16 [4096, 1024], P(('ctx', 'head')), may hold values from -12 to 12
- passage_v: bfloat16 [4096, 1024], P(('ctx', 'head')), may hold values from -6 to 6
- new_q: bfloat16 [2048, 16384], P(('ctx', 'head')), may hold values from -12 to 12
- new_k: bfloat16 [2048, 1024], P(('ctx', 'head')), may hold values from -12 to 12
- new_v: bfloat16 [2048, 1024], P(('ctx', 'head')), may hold values from -6 to 6
- segments: int32 [4096], replicated, may hold values from 0 to 15, never falling along the last dimension, each value on 1 to 512 neighbouring positions
Outputs:
- passage_out: bfloat16 [4096, 16384], P(('ctx', 'head'))
- new_out: bfloat16 [2048, 16384], P(('ctx', 'head'))
The draws below stay inside these ranges and needn't reach their ends.
Inputs may be any that keep to these rules, and one draw needn't show every extreme that they name: `segments`: passages are runs of equal numbers, rising by one from run to run, each of 1 to 512 tokens; some passage has exactly 512.
All inputs are finite; a program needn't handle non-finite values.
Results may differ from the reference program's by a relative error of at most 0.008.
Values may be sent and summed in bfloat16 or wider, within the bound.
A program may use at most 192 MiB of HBM per device.

```python
import math
import jax
import jax.numpy as jnp
import numpy as np
from jax import lax

QH = 128
KVH = 8
HD = 128
PT_DEV = 1024
MOST = 512
NEW = 2048
PTOK = 4096
PASSAGES = 16


def pair_draw(key, row_count, salt):
    base = jax.random.fold_in(key, salt)
    group_size = QH // KVH
    keys_main = jnp.clip(1.5 * jax.random.normal(jax.random.fold_in(base, 1), (row_count, KVH, HD), jnp.float32), -9.0, 9.0)
    query_main = jnp.clip(1.5 * jax.random.normal(jax.random.fold_in(base, 2), (row_count, KVH, group_size, HD), jnp.float32), -9.0, 9.0)
    return (query_main.reshape(row_count, QH * HD), keys_main.reshape(row_count, KVH * HD))


def draw_passage_q(key, part):
    return pair_draw(key, PTOK, 11)[0].astype(jnp.bfloat16)


def draw_passage_k(key, part):
    return pair_draw(key, PTOK, 11)[1].astype(jnp.bfloat16)


def draw_new_q(key, part):
    return pair_draw(key, NEW, 23)[0].astype(jnp.bfloat16)


def draw_new_k(key, part):
    return pair_draw(key, NEW, 23)[1].astype(jnp.bfloat16)


def block_levels(key, extent, split, smallest, top_value):
    level, own = 1.0, jax.random.fold_in(key, 6)
    for axis_at, blocks in split:
        draws = jnp.exp(jax.random.uniform(jax.random.fold_in(own, axis_at), (blocks,), jnp.float32, smallest / len(split), top_value / len(split)))
        level = level * jnp.repeat(draws, extent[axis_at] // blocks).reshape([-1 if axis == axis_at else 1 for axis in range(len(extent))])
    return level


def length_profile(count, total, bound, lean):
    weights = [(1 << 20) // math.isqrt(grade ** lean) + 1 for grade in range(2, count + 1)]
    surplus, counts = total - bound - (count - 1), [1] * (count - 1)
    while surplus > 0:
        free = [i for i in range(count - 1) if counts[i] < bound]
        pool, budget = sum([weights[i] for i in free]), surplus
        for i in free:
            addition = min(bound - counts[i], max(1, budget * weights[i] // pool), surplus)
            counts[i] = counts[i] + addition
            surplus = surplus - addition
    return np.array([bound] + counts)


def uneven_parts(own_key, count, total, most, skew):
    if count == 2:
        one = jax.random.randint(own_key, (), max(1, total - most), min(most, total - 1) + 1)
        return jnp.stack([one, total - one])
    sizes = jnp.asarray(length_profile(count, total, most, skew), jnp.int32)
    twos = (count - 1) // 2
    source_of, sink = sizes[1:1 + 2 * twos:2], sizes[2:2 + 2 * twos:2]
    room = jnp.minimum(source_of - 1, most - sink)
    moved = jax.random.randint(jax.random.fold_in(own_key, 1), (twos,), 0, 1 << 20) % (room + 1)
    sizes = sizes.at[1:1 + 2 * twos:2].set(source_of - moved).at[2:2 + 2 * twos:2].set(sink + moved)
    return sizes[jax.random.permutation(jax.random.fold_in(own_key, 2), count)]


def scatter_about(stream_key, dims, deviation, most, pieces=(), kind=jnp.bfloat16):
    entries = deviation * jax.random.normal(stream_key, dims, jnp.float32)
    if pieces:
        entries = entries * block_levels(stream_key, dims, pieces, -0.22, 0.18)
    return jnp.clip(entries, -most, most).astype(kind)


def setup_inputs(seed: int = 0) -> dict:
    splits = jax.random.split(jax.random.key(seed), 8)
    passage_q = draw_passage_q(jax.random.fold_in(splits[7], 71), 0)
    passage_k = draw_passage_k(jax.random.fold_in(splits[7], 71), 0)
    passage_v = scatter_about(splits[2], (PTOK, KVH * HD), 1.0, 6.0, ((0, 32),))
    new_q = draw_new_q(jax.random.fold_in(splits[7], 71), 0)
    new_k = draw_new_k(jax.random.fold_in(splits[7], 71), 0)
    new_v = scatter_about(splits[5], (NEW, KVH * HD), 1.0, 6.0, ((0, 32),))
    segments = jnp.searchsorted(jnp.cumsum(uneven_parts(splits[6], PASSAGES, PTOK, MOST, 2)), jnp.arange(PTOK), side="right").astype(jnp.int32)
    return {"passage_q": passage_q, "passage_k": passage_k, "passage_v": passage_v, "new_q": new_q, "new_k": new_k, "new_v": new_v, "segments": segments}


big_neg = -1.0e30


def soft_attend(scores, visible, values, form):
    masked = jnp.where(visible, scores, big_neg)
    row_max = jnp.max(masked, axis=-1, keepdims=True)
    weights = jnp.where(visible, jnp.exp(masked - row_max), 0.0)
    row_sum = jnp.sum(weights, axis=-1)
    rounded = lax.optimization_barrier(weights.astype(jnp.bfloat16)).astype(jnp.float32)
    weighted = jnp.einsum(form, rounded, values, precision=lax.Precision.HIGHEST)
    return (weighted / row_sum[..., None]).astype(jnp.bfloat16)


def reference(passage_q, passage_k, passage_v, new_q, new_k, new_v, segments):
    group_size = QH // KVH
    score_scale = HD ** -0.5
    block_rows = min(512, PT_DEV)
    pass_q = passage_q.reshape(PTOK, KVH, group_size, HD)
    pass_k = passage_k.reshape(PTOK, KVH, HD)
    pass_v = passage_v.reshape(PTOK, KVH, HD)
    keys_pad = jnp.concatenate([jnp.zeros((MOST, KVH, HD), jnp.bfloat16), pass_k], axis=0)
    vals_pad = jnp.concatenate([jnp.zeros((MOST, KVH, HD), jnp.bfloat16), pass_v], axis=0)
    seg_padded = jnp.concatenate([jnp.full((MOST,), -1, jnp.int32), segments.astype(jnp.int32)])

    def passage_block(block_id):
        first_row = (block_id * block_rows).astype(jnp.int32)
        q_block = lax.dynamic_slice_in_dim(pass_q, first_row, block_rows, 0).astype(jnp.float32)
        k_block = lax.dynamic_slice_in_dim(keys_pad, first_row, block_rows + MOST, 0).astype(jnp.float32)
        v_block = lax.dynamic_slice_in_dim(vals_pad, first_row, block_rows + MOST, 0).astype(jnp.float32)
        seg_query = lax.dynamic_slice_in_dim(seg_padded, first_row + MOST, block_rows, 0)
        seg_key = lax.dynamic_slice_in_dim(seg_padded, first_row, block_rows + MOST, 0)
        causal = jnp.arange(block_rows + MOST)[None, :] - MOST <= jnp.arange(block_rows)[:, None]
        visible = causal & (seg_query[:, None] == seg_key[None, :])
        scores = jnp.einsum('qjgd,kjd->qjgk', q_block, k_block, precision=lax.Precision.HIGHEST) * score_scale
        return soft_attend(scores, visible[:, None, None, :], v_block, 'qjgk,kjd->qjgd')

    passage_out = lax.map(passage_block, jnp.arange(PTOK // block_rows, dtype=jnp.int32))
    passage_out = passage_out.reshape(PTOK, QH * HD)

    new_block_rows = min(512, NEW)
    fresh_q = new_q.reshape(NEW, KVH, group_size, HD)
    keys_all = jnp.concatenate([pass_k, new_k.reshape(NEW, KVH, HD)], axis=0)
    vals_all = jnp.concatenate([pass_v, new_v.reshape(NEW, KVH, HD)], axis=0)
    keys_heads = jnp.transpose(keys_all, (1, 0, 2))
    vals_heads = jnp.transpose(vals_all, (1, 0, 2))

    def question_block(block_id):
        first_row = (block_id * new_block_rows).astype(jnp.int32)
        q_block = lax.dynamic_slice_in_dim(fresh_q, first_row, new_block_rows, 0)
        query_pos = first_row + jnp.arange(new_block_rows, dtype=jnp.int32)
        key_pos = jnp.arange(PTOK + NEW, dtype=jnp.int32)
        visible = (key_pos[None, :] < PTOK) | (key_pos[None, :] - PTOK <= query_pos[:, None])

        def per_head(inputs):
            q_head, k_head, v_head = inputs
            scores = jnp.einsum('qgd,kd->qgk', q_head.astype(jnp.float32), k_head.astype(jnp.float32), precision=lax.Precision.HIGHEST) * score_scale
            return soft_attend(scores, visible[:, None, :], v_head.astype(jnp.float32), 'qgk,kd->qgd')

        heads_out = lax.map(per_head, (jnp.transpose(q_block, (1, 0, 2, 3)), keys_heads, vals_heads))
        return jnp.transpose(heads_out, (1, 0, 2, 3))

    new_out = lax.map(question_block, jnp.arange(NEW // new_block_rows, dtype=jnp.int32))
    new_out = new_out.reshape(NEW, QH * HD)
    return passage_out, new_out
```

```python
import functools
import math

import jax
import jax.numpy as jnp
from jax import lax
from jax.experimental import pallas as pl
from jax.experimental.pallas import tpu as pltpu
from jax.sharding import Mesh, PartitionSpec as P

QH = 128
KVH = 8
HD = 128
MOST = 512
CORES = 2
NEG = -1e30
SCALE = HD ** -0.5 * math.log2(math.e)
DIMS_T = (((1,), (1,)), ((), ()))


def scores_of(q, k):
    return lax.dot_general(q, k, DIMS_T, preferred_element_type=jnp.float32)


def question_kernel(groups, key_block, z_ref, q_ref, pk_ref, pv_ref, nk_ref, nv_ref, o_ref, pva, nva, acc, top):
    rows = q_ref.shape[0]
    run = rows // groups
    passage = pk_ref.shape[0]
    span = nk_ref.shape[0] // groups

    @pl.when(pl.program_id(0) == 0)
    def _():
        pva[:, :HD] = pv_ref[...]
        pva[:, HD:] = jnp.ones((passage, HD), jnp.bfloat16)
        nva[:, :HD] = nv_ref[...]
        nva[:, HD:] = jnp.ones((span * groups, HD), jnp.bfloat16)

    jobs = [(pk_ref, pva, i * key_block, key_block, 0, False) for i in range(passage // key_block)]
    jobs += [(nk_ref, nva, b * span, span, b * run, True) for b in range(groups)]

    def scored(job):
        k_ref, _, at, size, first, own = job
        s = scores_of(q_ref[first:, :], k_ref[at:at + size, :])
        if own:
            here = lax.broadcasted_iota(jnp.int32, (run, size), 0) + z_ref[0] * run
            there = lax.broadcasted_iota(jnp.int32, (run, size), 1)
            edge = jnp.where(there <= here, s[:run], NEG)
            s = edge if first + run == rows else jnp.concatenate([edge, s[run:]], axis=0)
        return s

    s = scored(jobs[0])
    for i, job in enumerate(jobs):
        later = scored(jobs[i + 1]) if i + 1 < len(jobs) else None
        _, v_ref, at, size, first, own = job
        best = jnp.max(s, axis=1, keepdims=True)
        if i > 0:
            before = top[first:, :]
            best = jnp.maximum(before[:, :1], best)
        wide = jnp.broadcast_to(best, (rows - first, HD))
        p = jnp.exp2(s * SCALE - best * SCALE).astype(jnp.bfloat16)
        part = jnp.dot(p, v_ref[at:at + size, :], preferred_element_type=jnp.float32)
        if i > 0:
            shrink = jnp.exp2((before - wide) * SCALE)
            acc[first:, :HD] = acc[first:, :HD] * shrink + part[:, :HD]
            acc[first:, HD:] = acc[first:, HD:] * shrink + part[:, HD:]
        else:
            acc[...] = part
        top[first:, :] = wide
        s = later
    o_ref[...] = (acc[:, :HD] / acc[:, HD:]).astype(jnp.bfloat16)


def question_attention(z_index, q, pk, pv, nk, nv, groups):
    rows, columns = q.shape
    heads = columns // HD
    passage, new = pk.shape[0], nk.shape[0]
    key_block = 1024
    whole = lambda array: pl.BlockSpec(array.shape, lambda h: (0, 0))
    return pl.pallas_call(
        functools.partial(question_kernel, groups, key_block),
        grid=(heads,),
        in_specs=[
            pl.BlockSpec(memory_space=pltpu.SMEM),
            pl.BlockSpec((rows, HD), lambda h: (0, h)),
            whole(pk), whole(pv), whole(nk), whole(nv),
        ],
        out_specs=pl.BlockSpec((rows, HD), lambda h: (0, h)),
        out_shape=jax.ShapeDtypeStruct(q.shape, jnp.bfloat16),
        scratch_shapes=[
            pltpu.VMEM((passage, 2 * HD), jnp.bfloat16),
            pltpu.VMEM((new, 2 * HD), jnp.bfloat16),
            pltpu.VMEM((rows, 2 * HD), jnp.float32),
            pltpu.VMEM((rows, HD), jnp.float32),
        ],
        compiler_params=pltpu.CompilerParams(vmem_limit_bytes=48 * 2 ** 20),
        cost_estimate=pl.CostEstimate(
            flops=6 * rows * heads * HD * (passage + new // 2),
            bytes_accessed=8 * rows * columns,
            transcendentals=rows * heads * (passage + new // 2),
        ),
    )(z_index, q, pk, pv, nk, nv)


def passage_kernel(at_once, q_ref, k_ref, v_ref, sq_ref, sk_ref, o_ref, va, bias):
    rows = q_ref.shape[0]
    keys = k_ref.shape[0]
    heads = q_ref.shape[1] // HD

    @pl.when(pl.program_id(0) == 0)
    def _():
        here = lax.broadcasted_iota(jnp.int32, (rows, keys), 0) + (keys - rows)
        there = lax.broadcasted_iota(jnp.int32, (rows, keys), 1)
        seen = (there <= here) & (sq_ref[...] == sk_ref[...])
        bias[...] = jnp.where(seen, 0.0, NEG)
        va[:, HD:] = jnp.ones((keys, HD), jnp.bfloat16)

    va[:, :HD] = v_ref[...]

    def scored(g):
        q = jnp.concatenate([q_ref[:, h * HD:(h + 1) * HD] for h in range(g, g + at_once)], axis=0)
        return scores_of(q, k_ref[...])

    s = scored(0)
    for g in range(0, heads, at_once):
        later = scored(g + at_once) if g + at_once < heads else None
        s = (s.reshape(at_once, rows, keys) + bias[...][None]).reshape(at_once * rows, keys)
        best = jnp.max(s, axis=1, keepdims=True)
        p = jnp.exp2(s * SCALE - best * SCALE).astype(jnp.bfloat16)
        part = jnp.dot(p, va[...], preferred_element_type=jnp.float32)
        out = (part[:, :HD] / part[:, HD:]).astype(jnp.bfloat16)
        for h in range(at_once):
            o_ref[:, (g + h) * HD:(g + h + 1) * HD] = out[h * rows:(h + 1) * rows]
        s = later


def passage_attention(q, keys, values, seg_q, seg_k):
    rows = q.shape[0]
    window = keys.shape[0]
    share = QH // KVH * HD
    return pl.pallas_call(
        functools.partial(passage_kernel, 4),
        grid=(KVH,),
        in_specs=[
            pl.BlockSpec((rows, share), lambda j: (0, j)),
            pl.BlockSpec((window, HD), lambda j: (0, j)),
            pl.BlockSpec((window, HD), lambda j: (0, j)),
            pl.BlockSpec((rows, 1), lambda j: (0, 0)),
            pl.BlockSpec((1, window), lambda j: (0, 0)),
        ],
        out_specs=pl.BlockSpec((rows, share), lambda j: (0, j)),
        out_shape=jax.ShapeDtypeStruct(q.shape, jnp.bfloat16),
        scratch_shapes=[
            pltpu.VMEM((window, 2 * HD), jnp.bfloat16),
            pltpu.VMEM((rows, window), jnp.float32),
        ],
        compiler_params=pltpu.CompilerParams(vmem_limit_bytes=48 * 2 ** 20),
        cost_estimate=pl.CostEstimate(
            flops=6 * rows * QH * HD * window,
            bytes_accessed=4 * rows * QH * HD,
            transcendentals=rows * QH * window,
        ),
    )(q, keys, values, seg_q[:, None], seg_k[None, :])


def on_device(passage_q, passage_k, passage_v, new_q, new_k, new_v, segments):
    lines = lax.axis_size("line")
    plane = lax.axis_size("ctx") * CORES
    ctx_count = lax.axis_size("ctx")
    z_index = lax.axis_index("line")
    everyone = ("ctx", "line", "core")
    total = plane * lines
    flat = (lax.axis_index("ctx") * lines + z_index) * CORES + lax.axis_index("core")
    copies = plane // KVH
    prow, nrow = passage_k.shape[0], new_k.shape[0]

    def swap(array):
        return lax.all_to_all(array, ("ctx", "core"), split_axis=1, concat_axis=0, tiled=True)

    kv = jnp.concatenate(
        [jnp.concatenate([passage_k, new_k], axis=0).reshape(prow + nrow, KVH, HD),
         jnp.concatenate([passage_v, new_v], axis=0).reshape(prow + nrow, KVH, HD)], axis=2)
    kv = jnp.repeat(kv, copies, axis=1).reshape(prow + nrow, plane * 2 * HD)
    kv = swap(kv)
    q = swap(new_q)
    gathered = lax.all_gather(kv, "line", axis=0, tiled=True)
    gathered = gathered.reshape(lines, ctx_count, CORES, prow + nrow, 2 * HD)
    pk = gathered[:, :, :, :prow, :HD].reshape(-1, HD)
    pv = gathered[:, :, :, :prow, HD:].reshape(-1, HD)
    fresh = jnp.transpose(gathered[:, :, :, prow:, :], (1, 0, 2, 3, 4))
    nk = fresh[..., :HD].reshape(-1, HD)
    nv = fresh[..., HD:].reshape(-1, HD)

    hops = -(-(MOST - 1) // prow)
    pair = jnp.concatenate([passage_k, passage_v], axis=1)
    pieces = [
        lax.ppermute(pair, everyone, [(i - d, i) for i in range(d, total)]) for d in range(hops, 0, -1)
    ]
    around = jnp.concatenate(pieces + [pair], axis=0)
    window = hops * prow
    padded = jnp.concatenate([jnp.full((window,), -1, jnp.int32), segments])
    seg_k = lax.dynamic_slice_in_dim(padded, flat * prow, window + prow, 0)
    out_new = question_attention(z_index[None].astype(jnp.int32), q, pk, pv, nk, nv, ctx_count)
    out_new = lax.all_to_all(out_new, ("ctx", "core"), split_axis=0, concat_axis=1, tiled=True)
    out_pass = passage_attention(
        passage_q, around[:, :KVH * HD], around[:, KVH * HD:], seg_k[window:], seg_k)
    return out_pass, out_new


def solution(mesh):
    ctx, head = mesh.devices.shape
    finer = Mesh(mesh.devices.reshape(ctx, head // CORES, CORES), ("ctx", "line", "core"))
    split = P(("ctx", "line", "core"), None)
    return jax.shard_map(
        on_device, mesh=finer, in_specs=(split,) * 6 + (P(),), out_specs=(split, split), check_vma=False
    )
```

```python
import functools
import math

import jax
import jax.numpy as jnp
from jax import lax
from jax.experimental import pallas as pl
from jax.experimental.pallas import tpu as pltpu
from jax.sharding import Mesh, PartitionSpec as P

QH = 128
KVH = 8
HD = 128
MOST = 512
CORES = 2
NEG = -1e30
SCALE = HD ** -0.5 * math.log2(math.e)
DIMS_T = (((1,), (1,)), ((), ()))


def scores_of(q, k):
    return lax.dot_general(q, k, DIMS_T, preferred_element_type=jnp.float32)


def question_kernel(
    sizes, nq, pk, pv, nk, nv, out, around, kv, q, acc, top, bias, stage,
    kv_send, kv_recv, q_send, q_recv, line_send, line_recv, halo_send, halo_recv,
    relay_send, relay_recv, out_send, out_recv,
):
    ctx_count, lines, hops = sizes
    plane = ctx_count * CORES
    copies = plane // KVH
    prow, nrow = pk.shape[0], nk.shape[0]
    passage = plane * prow
    rows, width = q.shape
    heads = width // HD
    half = rows // 2
    run = CORES * nrow
    batch = 4
    total = plane * lines
    c, z, k = lax.axis_index("ctx"), lax.axis_index("line"), lax.axis_index("core")
    me = c * CORES + k
    flat = (c * lines + z) * CORES + k

    def peer(p):
        return (p // CORES, z, p % CORES)

    def flat_peer(f):
        return (f // (CORES * lines), f // CORES % lines, f % CORES)

    def remote(src, dst, send, recv, device):
        return pltpu.make_async_remote_copy(
            src_ref=src, dst_ref=dst, send_sem=send, recv_sem=recv,
            device_id=device, device_id_type=pl.DeviceIdType.MESH)

    def at(index, size):
        return pl.ds(pl.multiple_of(index * size, size), size)

    def kv_parts(p):
        column = at(p // copies, HD)
        old = at(me, prow)
        new = pl.ds(pl.multiple_of(passage + me * nrow, nrow), nrow)
        return [
            (pk.at[:, column], kv.at[z, old, 0:HD]),
            (pv.at[:, column], kv.at[z, old, HD:2 * HD]),
            (nk.at[:, column], kv.at[z, new, 0:HD]),
            (nv.at[:, column], kv.at[z, new, HD:2 * HD]),
        ]

    def kv_copies(step):
        p = (me + step) % plane
        return [remote(s, t, kv_send.at[step, n], kv_recv.at[step, n], peer(p))
                for n, (s, t) in enumerate(kv_parts(p))]

    def q_copy(step):
        p = (me + step) % plane
        return remote(nq.at[:, at(p, width)], q.at[at(me, nrow), :], q_send.at[step], q_recv.at[step], peer(p))

    own = [pltpu.make_async_copy(s, t, kv_recv.at[0, n]) for n, (s, t) in enumerate(kv_parts(me))]
    own += [pltpu.make_async_copy(nq.at[:, at(me, width)], q.at[at(me, nrow), :], q_recv.at[0])]
    wide = KVH * HD
    kept = [
        pltpu.make_async_copy(pk, around.at[hops * prow:(hops + 1) * prow, 0:wide], halo_recv.at[0, 0]),
        pltpu.make_async_copy(pv, around.at[hops * prow:(hops + 1) * prow, wide:2 * wide], halo_recv.at[0, 1]),
    ]

    def halo_copies(far):
        first = (hops - far) * prow
        device = flat_peer((flat + far) % total)
        return [
            remote(pk, around.at[first:first + prow, 0:wide], halo_send.at[far, 0], halo_recv.at[far, 0], device),
            remote(pv, around.at[first:first + prow, wide:2 * wide], halo_send.at[far, 1], halo_recv.at[far, 1], device),
        ]

    def relay(n):
        first = (hops - 2 * n - 1) * prow
        return remote(
            around.at[at(hops - 2 * n - 2 * k, prow), :], around.at[first:first + prow, :],
            relay_send.at[n], relay_recv.at[n], (c, z, 1 - k))

    def hop(side, step):
        ahead = 1 - 2 * side
        block = jnp.clip(z - ahead * (step - 1), 0, lines - 1)
        part = kv.at[block, :, 0:2 * HD]
        device = (c, (z + ahead + lines) % lines, k)
        return remote(part, part, line_send.at[side, step], line_recv.at[side, step], device)

    def sends(side, step):
        if side == 0:
            return (z - (step - 1) >= 0) & (z + 1 < lines)
        return (z + (step - 1) < lines) & (z >= 1)

    def receives(side, step):
        return z - step >= 0 if side == 0 else z + step < lines

    def out_copy(group, step):
        p = (me + step) % plane
        size = batch * HD
        return (stage.at[at(p, nrow), at(group, size)], out.at[:, at(me * (heads // batch) + group, size)], p)

    def out_remote(group, step):
        s, t, p = out_copy(group, step)
        return remote(s, t, out_send.at[group, step], out_recv.at[group, step], peer(p))

    def out_local(group):
        s, t, _ = out_copy(group, 0)
        return pltpu.make_async_copy(s, t, out_recv.at[group, 0])

    evens = range(2, hops + 1, 2)
    barrier = pltpu.get_barrier_semaphore()
    greeted = [peer((me + step) % plane) for step in range(1, plane)]
    greeted += [(c, (z + 1) % lines, k), (c, (z + lines - 1) % lines, k)]
    for far in evens:
        greeted += [flat_peer((flat + far) % total), flat_peer((flat + total - far) % total)]
    for device in greeted:
        pl.semaphore_signal(barrier, inc=1, device_id=device, device_id_type=pl.DeviceIdType.MESH)
    pl.semaphore_wait(barrier, len(greeted))

    for step in range(1, plane):
        for copy in kv_copies(step):
            copy.start()
    for copy in own:
        copy.start()
    for step in range(1, plane):
        q_copy(step).start()
    for copy in halo_copies(2) + kept:
        copy.start()

    def clear(h, _):
        acc[h] = jnp.zeros((rows, 2 * HD), jnp.float32)
        top[h] = jnp.full((rows, HD), NEG, jnp.float32)
        return 0

    lax.fori_loop(0, heads, clear, 0)
    for line in range(lines):
        kv[line, :, 2 * HD:] = jnp.ones((kv.shape[1], HD), jnp.bfloat16)

    def exchange(phase):
        for side in range(2):
            @pl.when((phase >= 1) & receives(side, phase))
            def _():
                hop(side, phase).wait_recv()
        for side in range(2):
            @pl.when((phase + 1 < lines) & sends(side, phase + 1))
            def _():
                hop(side, phase + 1).start()

    def turn(phase):
        near = jnp.minimum(z, lines - 1 - z)
        both = phase <= 2 * near
        distance = jnp.where(both, (phase + 1) // 2, phase - near)
        left = jnp.where(both, phase % 2 == 1, z > near)
        return jnp.where(phase == 0, z, jnp.where(left, z - distance, z + distance))

    def masks(block):
        row = lax.broadcasted_iota(jnp.int32, (rows, rows), 0)
        col = lax.broadcasted_iota(jnp.int32, (rows, rows), 1)
        step = (lines - 1) * run
        here = row + row // run * step + z * run
        there = col + col // run * step + block * run
        bias[...] = jnp.where(there <= here, 0.0, NEG)

    def head_block(h, block, last):
        lane = at(h, HD)
        scored = []
        for part in range(2):
            first, new = part * half, (part + 1) * half
            qs = q[first:first + half, lane]
            old_s = scores_of(qs, kv[block, 0:passage, 0:HD])
            new_s = scores_of(qs, kv[block, passage:passage + new, 0:HD]) + bias[first:first + half, 0:new]
            scored.append((first, new, old_s, new_s))
        for first, new, old_s, new_s in scored:
            before = top[h, first:first + half, :]
            best = jnp.maximum(jnp.max(old_s, axis=1, keepdims=True), jnp.max(new_s, axis=1, keepdims=True))
            best = jnp.maximum(before[:, :1], best)
            spread = jnp.broadcast_to(best, (half, HD))
            old_p = jnp.exp2(old_s * SCALE - best * SCALE).astype(jnp.bfloat16)
            new_p = jnp.exp2(new_s * SCALE - best * SCALE).astype(jnp.bfloat16)
            got = jnp.dot(old_p, kv[block, 0:passage, HD:3 * HD], preferred_element_type=jnp.float32)
            got += jnp.dot(new_p, kv[block, passage:passage + new, HD:3 * HD], preferred_element_type=jnp.float32)
            shrink = jnp.exp2((before - spread) * SCALE)
            num = acc[h, first:first + half, 0:HD] * shrink + got[:, :HD]
            den = acc[h, first:first + half, HD:2 * HD] * shrink + got[:, HD:]
            if last:
                stage[first:first + half, lane] = (num / den).astype(jnp.bfloat16)
            else:
                acc[h, first:first + half, 0:HD] = num
                acc[h, first:first + half, HD:2 * HD] = den
                top[h, first:first + half, :] = spread

    for copy in own[:4]:
        copy.wait()
    for step in range(1, plane):
        for copy in kv_copies(step):
            copy.wait_recv()

    def phase_step(phase, _):
        exchange(phase)

        @pl.when(phase == 0)
        def _():
            own[4].wait()
            for step in range(1, plane):
                q_copy(step).wait_recv()

        @pl.when(phase == lines - 2)
        def _():
            for far in evens[1:]:
                for copy in halo_copies(far):
                    copy.start()

        block = turn(phase)
        masks(block)

        def each(h, _):
            head_block(h, block, False)
            return 0

        lax.fori_loop(0, heads, each, 0)
        return 0

    lax.fori_loop(0, lines - 1, phase_step, 0)
    exchange(lines - 1)
    block = turn(lines - 1)
    masks(block)
    groups = heads // batch

    def finish(group, _):
        @pl.when(group == groups - 1)
        def _():
            for copy in kept:
                copy.wait()
            for far in evens:
                for copy in halo_copies(far):
                    copy.wait_recv()
            for n in range(hops // 2):
                relay(n).start()

        def each(i, _):
            head_block(group * batch + i, block, True)
            return 0

        lax.fori_loop(0, batch, each, 0)
        for step in range(1, plane):
            out_remote(group, step).start()
        out_local(group).start()
        return 0

    lax.fori_loop(0, groups, finish, 0)

    for step in range(1, plane):
        for copy in kv_copies(step):
            copy.wait_send()
        q_copy(step).wait_send()
    for step in range(1, lines):
        for side in range(2):
            @pl.when(sends(side, step))
            def _():
                hop(side, step).wait_send()
    for far in evens:
        for copy in halo_copies(far):
            copy.wait_send()
    for n in range(hops // 2):
        relay(n).wait()

    def drain(group, _):
        out_local(group).wait()
        for step in range(1, plane):
            out_remote(group, step).wait()
        return 0

    lax.fori_loop(0, groups, drain, 0)


def question_attention(sizes, nq, pk, pv, nk, nv):
    ctx_count, lines, hops = sizes
    plane = ctx_count * CORES
    prow, nrow = pk.shape[0], nk.shape[0]
    width = nq.shape[1] // plane
    rows, heads = plane * nrow, width // HD
    keys = lines * plane * (prow + nrow)
    groups = heads // 4
    dma = pltpu.SemaphoreType.DMA
    anywhere = pl.BlockSpec(memory_space=pl.ANY)
    return pl.pallas_call(
        functools.partial(question_kernel, sizes),
        in_specs=[anywhere] * 5,
        out_specs=[anywhere] * 2,
        out_shape=[
            jax.ShapeDtypeStruct(nq.shape, jnp.bfloat16),
            jax.ShapeDtypeStruct(((hops + 1) * prow, 2 * KVH * HD), jnp.bfloat16),
        ],
        scratch_shapes=[
            pltpu.VMEM((lines, plane * (prow + nrow), 3 * HD), jnp.bfloat16),
            pltpu.VMEM((rows, width), jnp.bfloat16),
            pltpu.VMEM((heads, rows, 2 * HD), jnp.float32),
            pltpu.VMEM((heads, rows, HD), jnp.float32),
            pltpu.VMEM((rows, rows), jnp.float32),
            pltpu.VMEM((rows, width), jnp.bfloat16),
            dma((plane, 4)), dma((plane, 4)), dma((plane,)), dma((plane,)),
            dma((2, lines)), dma((2, lines)), dma((hops + 1, 2)), dma((hops + 1, 2)),
            dma((hops // 2,)), dma((hops // 2,)), dma((groups, plane)), dma((groups, plane)),
        ],
        compiler_params=pltpu.CompilerParams(
            vmem_limit_bytes=56 * 2 ** 20, collective_id=0, has_side_effects=True),
        cost_estimate=pl.CostEstimate(
            flops=6 * rows * heads * HD * keys, bytes_accessed=8 * rows * width,
            transcendentals=rows * heads * keys),
    )(nq, pk, pv, nk, nv)


def passage_kernel(at_once, q_ref, k_ref, v_ref, sq_ref, sk_ref, o_ref, va, bias):
    rows = q_ref.shape[0]
    keys = k_ref.shape[0]
    heads = q_ref.shape[1] // HD

    @pl.when(pl.program_id(0) == 0)
    def _():
        here = lax.broadcasted_iota(jnp.int32, (rows, keys), 0) + (keys - rows)
        there = lax.broadcasted_iota(jnp.int32, (rows, keys), 1)
        seen = (there <= here) & (sq_ref[...] == sk_ref[...])
        bias[...] = jnp.where(seen, 0.0, NEG)
        va[:, HD:] = jnp.ones((keys, HD), jnp.bfloat16)

    va[:, :HD] = v_ref[...]

    def scored(g):
        q = jnp.concatenate([q_ref[:, h * HD:(h + 1) * HD] for h in range(g, g + at_once)], axis=0)
        return scores_of(q, k_ref[...])

    s = scored(0)
    for g in range(0, heads, at_once):
        later = scored(g + at_once) if g + at_once < heads else None
        s = (s.reshape(at_once, rows, keys) + bias[...][None]).reshape(at_once * rows, keys)
        best = jnp.max(s, axis=1, keepdims=True)
        p = jnp.exp2(s * SCALE - best * SCALE).astype(jnp.bfloat16)
        part = jnp.dot(p, va[...], preferred_element_type=jnp.float32)
        out = (part[:, :HD] / part[:, HD:]).astype(jnp.bfloat16)
        for h in range(at_once):
            o_ref[:, (g + h) * HD:(g + h + 1) * HD] = out[h * rows:(h + 1) * rows]
        s = later


def passage_attention(q, around, seg_q, seg_k):
    rows = q.shape[0]
    window = around.shape[0]
    share = QH // KVH * HD
    return pl.pallas_call(
        functools.partial(passage_kernel, 4),
        grid=(KVH,),
        in_specs=[
            pl.BlockSpec((rows, share), lambda j: (0, j)),
            pl.BlockSpec((window, HD), lambda j: (0, j)),
            pl.BlockSpec((window, HD), lambda j: (0, KVH + j)),
            pl.BlockSpec((rows, 1), lambda j: (0, 0)),
            pl.BlockSpec((1, window), lambda j: (0, 0)),
        ],
        out_specs=pl.BlockSpec((rows, share), lambda j: (0, j)),
        out_shape=jax.ShapeDtypeStruct(q.shape, jnp.bfloat16),
        scratch_shapes=[
            pltpu.VMEM((window, 2 * HD), jnp.bfloat16),
            pltpu.VMEM((rows, window), jnp.float32),
        ],
        compiler_params=pltpu.CompilerParams(vmem_limit_bytes=48 * 2 ** 20),
        cost_estimate=pl.CostEstimate(
            flops=6 * rows * QH * HD * window,
            bytes_accessed=4 * rows * QH * HD,
            transcendentals=rows * QH * window,
        ),
    )(q, around, around, seg_q[:, None], seg_k[None, :])


def on_device(passage_q, passage_k, passage_v, new_q, new_k, new_v, segments):
    lines = lax.axis_size("line")
    ctx_count = lax.axis_size("ctx")
    prow = passage_k.shape[0]
    flat = (lax.axis_index("ctx") * lines + lax.axis_index("line")) * CORES + lax.axis_index("core")
    hops = -(-(MOST - 1) // prow)
    hops += hops % 2
    window = hops * prow
    padded = jnp.concatenate([jnp.full((window,), -1, jnp.int32), segments])
    seg_k = lax.dynamic_slice_in_dim(padded, flat * prow, window + prow, 0)
    out_new, around = question_attention(
        (ctx_count, lines, hops), new_q, passage_k, passage_v, new_k, new_v)
    out_pass = passage_attention(passage_q, around, seg_k[window:], seg_k)
    return out_pass, out_new


def solution(mesh):
    ctx, head = mesh.devices.shape
    finer = Mesh(mesh.devices.reshape(ctx, head // CORES, CORES), ("ctx", "line", "core"))
    split = P(("ctx", "line", "core"), None)
    return jax.shard_map(
        on_device, mesh=finer, in_specs=(split,) * 6 + (P(),), out_specs=(split, split), check_vma=False
    )
```
